32 devices in a mesh: dp: 8 (over z, y), tensor: 4 (over x, core).
Axes of the slice: x: 2, y: 2, z: 4, core: 2. Of those that a mesh axis runs over, the one named last changes fastest.
Arguments:
- cotangent: bfloat16 [4096, 4608], P(('dp', 'tensor')), may hold values from -6 to 6
- attn_saved: bfloat16 [4096, 2048], P('dp', 'tensor'), may hold values from -6 to 6
- attn_next: bfloat16 [4096, 2048], P('dp', 'tensor'), may hold values from -6 to 6
- weight: bfloat16 [4608, 2048], P('dp', 'tensor'), may hold values from -0.125 to 0.125
- moment1: float32 [4608, 2048], P('dp', 'tensor'), may hold values from -6 to 6
- moment2: float32 [4608, 2048], P('dp', 'tensor'), may hold values from 0.1 to 10
Outputs:
- grad_attn: bfloat16 [4096, 2048], P('dp', 'tensor')
- new_weight: bfloat16 [4608, 2048], P('dp', 'tensor')
- new_moment1: float32 [4608, 2048], P('dp', 'tensor')
- new_moment2: float32 [4608, 2048], P('dp', 'tensor')
- next_out: bfloat16 [4096, 4608], P(('dp', 'tensor'))
The draws below stay inside these ranges and needn't reach their ends.
All inputs are finite; a program needn't handle non-finite values.
Results may differ from the reference program's by a relative error of at most 0.013.
Values may be sent and summed in bfloat16 or wider, within the bound.
No kernel may reach another device: no remote copies, remote signals or barrier semaphores. Data moves between devices by JAX's collectives and lax.ppermute only.
A program may use at most 128 MiB of HBM per device.

```python
import math
import jax
import jax.numpy as jnp
from jax import lax

D = 4608
HQ = 2048
TOKENS = 4096
N_TENSOR = 4


def spiked(array, key, source, target, blocks, factor):
    owner, partner = [(jnp.arange(array.shape[position]) // (array.shape[position] // blocks)).reshape([-1 if axis == position else 1 for axis in range(array.ndim)]) for position in (source, target)]
    chosen = jax.random.permutation(key, blocks)[partner]
    strong = (owner == chosen) | (owner == (partner + blocks // 2) % blocks)
    return jnp.where(strong, factor * array, array)


def level_of(own_key, extent, shards, smallest, high):
    level, own = 1.0, jax.random.fold_in(own_key, 6)
    for axis_at, parts in shards:
        draws = jnp.exp(jax.random.uniform(jax.random.fold_in(own, axis_at), (parts,), jnp.float32, smallest / len(shards), high / len(shards)))
        level = level * jnp.repeat(draws, extent[axis_at] // parts).reshape([-1 if axis == axis_at else 1 for axis in range(len(extent))])
    return level


def gaussian(own_key, extent, width, limit, pieces=(), kind=jnp.bfloat16):
    entries = width * jax.random.normal(own_key, extent, jnp.float32)
    if pieces:
        entries = entries * level_of(own_key, extent, pieces, -0.22, 0.18)
    return jnp.clip(entries, -limit, limit).astype(kind)


def noise_with(own_key, dims, deviation, bound, cuts, heavy, held_as=jnp.bfloat16):
    result = deviation * jax.random.normal(own_key, dims, jnp.float32)
    if cuts:
        result = result * level_of(own_key, dims, cuts, -0.22, 0.18)
    return jnp.clip(spiked(result, jax.random.fold_in(own_key, 3), *heavy), -bound, bound).astype(held_as)


def setup_inputs(seed: int = 0) -> dict:
    splits = jax.random.split(jax.random.key(seed), 7)
    cotangent = noise_with(splits[0], (TOKENS, D), 1.0, 6.0, ((0, 32),), (0, 1, 32, 2.75))
    attn_saved = gaussian(splits[1], (TOKENS, HQ), 1.0, 6.0, ((0, 8), (1, 4)))
    attn_next = gaussian(splits[2], (TOKENS, HQ), 1.0, 6.0, ((0, 8), (1, 4)))
    weight = gaussian(splits[3], (D, HQ), HQ ** -0.5, 0.125, ((0, 8), (1, 4)))
    moment1 = gaussian(splits[4], (D, HQ), 1.0, 6.0, ((0, 8), (1, 4)), jnp.float32)
    moment2 = jnp.clip(jnp.exp(math.log(10.0) - 4.6051702 * jax.random.uniform(splits[5], (D, HQ), jnp.float32) ** level_of(splits[5], (D, HQ), ((0, 8), (1, 4)), -0.2, 0.2)), 0.1, 10.0)
    return dict(cotangent=cotangent, attn_saved=attn_saved, attn_next=attn_next, weight=weight, moment1=moment1, moment2=moment2)


first_decay = 0.9
second_decay = 0.95
first_fix = 1.0 - 0.9 ** 10
second_fix = 1.0 - 0.95 ** 10
learning_rate = 0.002
weight_decay = 0.1
epsilon = 1e-08

def reference(cotangent, attn_saved, attn_next, weight, moment1, moment2):
    gradient = lax.dot_general(cotangent, attn_saved, (((0,), (0,)), ((), ())), preferred_element_type=jnp.float32)
    gradient = gradient * (1.0 / math.sqrt(TOKENS))
    grad_attn = jnp.dot(cotangent, weight, preferred_element_type=jnp.float32).astype(jnp.bfloat16)
    new_moment1 = first_decay * moment1 + (1.0 - first_decay) * gradient
    new_moment2 = second_decay * moment2 + (1.0 - second_decay) * gradient * gradient
    update = new_moment1 / first_fix / (jnp.sqrt(new_moment2 / second_fix) + epsilon)
    new_weight = (weight.astype(jnp.float32) * (1.0 - learning_rate * weight_decay) - learning_rate * update).astype(jnp.bfloat16)
    group_width = HQ // N_TENSOR
    next_out = jnp.zeros((TOKENS, D), jnp.float32)
    for head_group in range(N_TENSOR):
        lower = head_group * group_width
        product = lax.dot_general(attn_next[:, lower:lower + group_width], new_weight[:, lower:lower + group_width], (((1,), (1,)), ((), ())), preferred_element_type=jnp.float32)
        rounded = lax.optimization_barrier(product.astype(jnp.bfloat16))
        next_out = next_out + rounded.astype(jnp.float32)
    return (grad_attn, new_weight, new_moment1, new_moment2, next_out.astype(jnp.bfloat16))
```

```python
import functools
import math

import jax
import jax.numpy as jnp
from jax import lax
from jax.experimental import pallas as pl
from jax.experimental.pallas import tpu as pltpu
from jax.sharding import PartitionSpec as P

first_decay = 0.9
second_decay = 0.95
first_fix = 1.0 - 0.9**10
second_fix = 1.0 - 0.95**10
learning_rate = 0.002
weight_decay = 0.1
epsilon = 1e-08
bf16 = jnp.bfloat16
f32 = jnp.float32
VMEM_LIMIT = 48 * 2**20


def adamw_step(gradient, weight, moment1, moment2):
    new_moment1 = first_decay * moment1 + (1.0 - first_decay) * gradient
    new_moment2 = second_decay * moment2 + (1.0 - second_decay) * gradient * gradient
    update = new_moment1 / first_fix / (jnp.sqrt(new_moment2 / second_fix) + epsilon)
    new_weight = (
        weight.astype(f32) * (1.0 - learning_rate * weight_decay) - learning_rate * update
    ).astype(bf16)
    return (new_weight, new_moment1, new_moment2)


def flip(value, axis, bit):
    return lax.ppermute(value, axis, [(i, i ^ bit) for i in range(lax.axis_size(axis))])


def to_partner(value):
    return flip(value, "dp", 1)


def to_chip(value):
    return flip(value, "tensor", 2)


def to_core(value):
    return flip(value, "tensor", 1)


def up(value, step, n):
    pairs = [(2 * z + y, 2 * z + 2 + y) for z in range(n - 1) for y in range(2) if step(z)]
    return lax.ppermute(value, "dp", pairs)


def down(value, step, n):
    pairs = [(2 * z + 2 + y, 2 * z + y) for z in range(n - 1) for y in range(2) if step(n - 2 - z)]
    return lax.ppermute(value, "dp", pairs)


def stage(*values):
    return lax.optimization_barrier(values)


def arrivals(n):
    table = []
    for z in range(n):
        steps = [(d, s) for s in range(1, n) for d in (1, -1) if 0 <= z - d * s < n]
        table.append(steps)
    return table


def pick(z, choices):
    result, seen = choices[-1], [choices[-1]]
    for value in reversed(choices):
        if not any(value is other for other in seen):
            seen.append(value)
            hit = functools.reduce(jnp.logical_or, [z == j for j, v in enumerate(choices) if v is value])
            result = jnp.where(hit, value, result)
    return result


def relative(rows, x, c):
    block = rows.shape[0] // 4
    rows = rows.reshape(2, 2, block, rows.shape[1])
    rows = jnp.where(x == 1, rows[::-1], rows)
    rows = jnp.where(c == 1, rows[:, ::-1], rows)
    return rows.transpose(1, 0, 2, 3).reshape(4 * block, -1)


def absolute(rows, x, c):
    block = rows.shape[0] // 4
    rows = rows.reshape(2, 2, block, -1).transpose(1, 0, 2, 3)
    rows = jnp.where(c == 1, rows[:, ::-1], rows)
    rows = jnp.where(x == 1, rows[::-1], rows)
    return rows.reshape(4 * block, -1)


def params():
    return pltpu.CompilerParams(vmem_limit_bytes=VMEM_LIMIT)


def cost(flops, bytes_accessed):
    return pl.CostEstimate(flops=flops, bytes_accessed=bytes_accessed, transcendentals=0)


def gradient_kernel(scale, *refs):
    pieces, (saved0, saved1, out) = refs[:8], refs[8:]
    rows = saved0.shape[0]
    left = jnp.concatenate([ref[0] for ref in pieces], axis=1)
    total = jnp.dot(left[:, :rows], saved0[...], preferred_element_type=f32)
    total += jnp.dot(left[:, rows:], saved1[...], preferred_element_type=f32)
    out[0] = (total * scale).astype(bf16)


def gradient_part(pieces, saved0, saved1, first, count, scale):
    _, own, tok = pieces[0].shape
    rows, wide = saved0.shape
    whole = pl.BlockSpec((rows, wide), lambda i: (0, 0))
    return pl.pallas_call(
        functools.partial(gradient_kernel, scale),
        grid=(count,),
        in_specs=[pl.BlockSpec((1, own, tok), lambda i: (i + first, 0, 0))] * 8 + [whole] * 2,
        out_specs=pl.BlockSpec((1, own, wide), lambda i: (i, 0, 0)),
        out_shape=jax.ShapeDtypeStruct((count, own, wide), bf16),
        compiler_params=params(),
        cost_estimate=cost(2 * count * own * 2 * rows * wide, 2 * count * own * (2 * rows + wide) + 4 * rows * wide),
        name="gradient_part",
    )(*pieces, saved0, saved1)


def attn_kernel(*refs):
    pieces, (weights, kept, sent, total) = refs[:8], refs[8:]
    step = pl.program_id(0)
    rows = kept.shape[0]
    left = jnp.concatenate([ref[0] for ref in pieces], axis=1)
    product = lax.dot_general(left, weights[0], (((0,), (0,)), ((), ())), preferred_element_type=f32)

    @pl.when(step == 0)
    def _():
        total[...] = product

    @pl.when(step > 0)
    def _():
        total[...] += product

    @pl.when(step == pl.num_programs(0) - 1)
    def _():
        kept[...] = total[:rows]
        sent[...] = total[rows:].astype(bf16)


def attn_part(pieces, weights):
    n, own, tok = pieces[0].shape
    wide = weights.shape[2]
    rows = 4 * tok
    whole = pl.BlockSpec((rows, wide), lambda i: (0, 0))
    return pl.pallas_call(
        attn_kernel,
        grid=(n,),
        in_specs=[pl.BlockSpec((1, own, tok), lambda i: (i, 0, 0))] * 8
        + [pl.BlockSpec((1, own, wide), lambda i: (i, 0, 0))],
        out_specs=[whole, whole],
        out_shape=[jax.ShapeDtypeStruct((rows, wide), f32), jax.ShapeDtypeStruct((rows, wide), bf16)],
        scratch_shapes=[pltpu.VMEM((2 * rows, wide), f32)],
        compiler_params=params(),
        cost_estimate=cost(4 * n * own * rows * wide, 2 * n * own * (2 * rows + wide) + 6 * rows * wide),
        name="attn_part",
    )(*pieces, weights)


def outward_kernel(block, next0, next1, kept, sent):
    tok = kept.shape[3]
    for y, following in enumerate((next0, next1)):
        out = lax.dot_general(
            block[...], following[...], (((1,), (1,)), ((), ())), preferred_element_type=f32
        ).astype(bf16)
        for chip in range(2):
            kept[chip, y] = out[:, chip * tok : (chip + 1) * tok]
            sent[chip, y] = out[:, (2 + chip) * tok : (3 + chip) * tok]


def outward_part(block, next0, next1):
    own, wide = block.shape
    rows = next0.shape[0]
    shape = jax.ShapeDtypeStruct((2, 2, own, rows // 4), bf16)
    return pl.pallas_call(
        outward_kernel,
        out_shape=[shape, shape],
        compiler_params=params(),
        cost_estimate=cost(4 * own * rows * wide, 2 * (own * wide + 2 * rows * wide + 2 * own * rows)),
        name="outward_part",
    )(block, next0, next1)


def add(a, b):
    return (a.astype(f32) + b.astype(f32)).astype(bf16)


def local(cotangent, attn_saved, attn_next, weight, moment1, moment2):
    dp, t = lax.axis_index("dp"), lax.axis_index("tensor")
    n = lax.axis_size("dp") // 2
    z, y, x, c = dp // 2, dp % 2, t // 2, t % 2
    own, wide = weight.shape
    tok = cotangent.shape[0]
    scale = 1.0 / math.sqrt(4 * tok * lax.axis_size("dp"))
    order = [r for k in range(1, n // 2 + 1) for r in dict.fromkeys((k, n - k))] + [0]
    half = n // 2

    blocks = cotangent.T.reshape(n, 2, own, tok)
    blocks = jnp.take(blocks, (z + jnp.array(order)) % n, axis=0)
    mine = jnp.where(y == 0, blocks[:, 0], blocks[:, 1])
    other = jnp.where(y == 0, blocks[:, 1], blocks[:, 0])
    saved0 = relative(attn_saved, x, c)

    weights = {(1, 0): weight, (-1, 0): weight}

    def weight_step(s):
        weights[1, s] = up(weights[1, s - 1], lambda a: a >= s - 1, n)
        weights[-1, s] = down(weights[-1, s - 1], lambda a: a >= s - 1, n)

    other, mine, weight0 = stage(other, mine, weight)
    weights[1, 0] = weights[-1, 0] = weight0
    partner = to_partner(other)
    mine_x = to_chip(mine)
    mine_c = to_core(mine)
    weight_step(1)
    partner, mine_x, mine_c, weights[1, 1], weights[-1, 1], saved0 = stage(
        partner, mine_x, mine_c, weights[1, 1], weights[-1, 1], saved0
    )
    saved1 = to_partner(saved0)
    partner_x = to_chip(partner)
    partner_c = to_core(partner)
    mine_xc = to_core(mine_x)
    if n > 2:
        weight_step(2)
    else:
        weights[1, 2] = weights[-1, 2] = weight
    saved1, partner_x, partner_c, mine_xc, weights[1, 2], weights[-1, 2] = stage(
        saved1, partner_x, partner_c, mine_xc, weights[1, 2], weights[-1, 2]
    )
    partner_xc = to_core(partner_x)
    pieces = [mine, mine_x, mine_c, mine_xc, partner, partner_x, partner_c, partner_xc]

    first = gradient_part(pieces, saved0, saved1, 0, half, scale)
    parts = {r: first[j] for j, r in enumerate(order[:half])}
    next0 = relative(attn_next, x, c)

    rising, falling = parts[n - 1], parts[1]
    for s in range(1, n):
        rising = up(rising, lambda a: a <= s - 1, n)
        falling = down(falling, lambda a: a <= s - 1, n)
        if s == 1:
            next1 = to_partner(next0)
            second = gradient_part(pieces, saved0, saved1, half, n - half, scale)
            rising, falling, next1, second = stage(rising, falling, next1, second)
            parts.update({r: second[j] for j, r in enumerate(order[half:])})
        if s + 2 < n:
            weight_step(s + 2)
            rising, falling, weights[1, s + 2], weights[-1, s + 2] = stage(
                rising, falling, weights[1, s + 2], weights[-1, s + 2]
            )
        if s == n - 2:
            gathered = jnp.stack(
                [jnp.where(z >= n - r, weights[1, n - r], weights[-1, r]) if r else weight for r in order]
            )
            kept, sent = attn_part(pieces, gathered)
            rising, falling, kept, sent = stage(rising, falling, kept, sent)
        if s < n - 1:
            rising = add(rising, parts[n - s - 1])
            falling = add(falling, parts[s + 1])
    sent = to_partner(sent)
    rising, falling, sent = stage(rising, falling, sent)
    gradient = parts[0].astype(f32) + rising.astype(f32) + falling.astype(f32)
    new_weight, new_moment1, new_moment2 = adamw_step(gradient, weight, moment1, moment2)
    grad_attn = absolute((kept + sent.astype(f32)).astype(bf16), x, c)

    table = arrivals(n)
    news = {(1, 0): new_weight, (-1, 0): new_weight}
    block, results, pending = new_weight, [], None
    for s in range(1, n + 1):
        if s < n:
            news[1, s] = up(news[1, s - 1], lambda a: a >= s - 1, n)
            news[-1, s] = down(news[-1, s - 1], lambda a: a >= s - 1, n)
        kept, sent = outward_part(block, next0, next1)
        half_sum = add(kept, to_core(sent))
        sums = add(half_sum[0], to_chip(half_sum[1]))
        if pending is not None:
            results.append((pending[0], to_partner(pending[1])))
        if s < n:
            sums, news[1, s], news[-1, s] = stage(sums, news[1, s], news[-1, s])
            block = pick(z, [news[steps[s - 1]] for steps in table])
        pending = sums
    results.append((pending[0], to_partner(pending[1])))

    mine = jnp.stack([m for m, _ in results])
    other = jnp.stack([o for _, o in results])
    halves = jnp.stack([jnp.where(y == 0, mine, other), jnp.where(y == 0, other, mine)], axis=1)
    slots = [[0] * n for _ in range(n)]
    for plane in range(n):
        for k, (d, s) in enumerate(table[plane]):
            slots[plane][plane - d * s] = k + 1
    next_out = jnp.take(halves, jnp.array(slots)[z], axis=0).reshape(2 * n * own, tok).T
    return (grad_attn, new_weight, new_moment1, new_moment2, next_out)


def solution(mesh):
    return jax.shard_map(
        local,
        mesh=mesh,
        in_specs=(
            P(("dp", "tensor"), None),
            P("dp", "tensor"),
            P("dp", "tensor"),
            P("dp", "tensor"),
            P("dp", "tensor"),
            P("dp", "tensor"),
        ),
        out_specs=(
            P("dp", "tensor"),
            P("dp", "tensor"),
            P("dp", "tensor"),
            P("dp", "tensor"),
            P(("dp", "tensor"), None),
        ),
        check_vma=False,
    )
```

```python
import functools
import math

import jax
import jax.numpy as jnp
from jax import lax
from jax.experimental import pallas as pl
from jax.experimental.pallas import tpu as pltpu
from jax.sharding import PartitionSpec as P

first_decay = 0.9
second_decay = 0.95
first_fix = 1.0 - 0.9**10
second_fix = 1.0 - 0.95**10
learning_rate = 0.002
weight_decay = 0.1
epsilon = 1e-08
bf16 = jnp.bfloat16
f32 = jnp.float32
VMEM_LIMIT = 48 * 2**20


def adamw_step(gradient, weight, moment1, moment2):
    new_moment1 = first_decay * moment1 + (1.0 - first_decay) * gradient
    new_moment2 = second_decay * moment2 + (1.0 - second_decay) * gradient * gradient
    update = new_moment1 / first_fix / (jnp.sqrt(new_moment2 / second_fix) + epsilon)
    new_weight = (
        weight.astype(f32) * (1.0 - learning_rate * weight_decay) - learning_rate * update
    ).astype(bf16)
    return (new_weight, new_moment1, new_moment2)


def flip(value, axis, bit):
    return lax.ppermute(value, axis, [(i, i ^ bit) for i in range(lax.axis_size(axis))])


def to_partner(value):
    return flip(value, "dp", 1)


def to_chip(value):
    return flip(value, "tensor", 2)


def to_core(value):
    return flip(value, "tensor", 1)


def to_plane(value, bit):
    return flip(value, "dp", 2 * bit)


def stage(*values):
    return lax.optimization_barrier(values)


def relative(rows, x, c):
    block = rows.shape[0] // 4
    rows = rows.reshape(2, 2, block, rows.shape[1])
    rows = jnp.where(x == 1, rows[::-1], rows)
    rows = jnp.where(c == 1, rows[:, ::-1], rows)
    return rows.transpose(1, 0, 2, 3).reshape(4 * block, -1)


def absolute(rows, x, c):
    block = rows.shape[0] // 4
    rows = rows.reshape(2, 2, block, -1).transpose(1, 0, 2, 3)
    rows = jnp.where(c == 1, rows[:, ::-1], rows)
    rows = jnp.where(x == 1, rows[::-1], rows)
    return rows.reshape(4 * block, -1)


def params():
    return pltpu.CompilerParams(vmem_limit_bytes=VMEM_LIMIT)


def cost(flops, bytes_accessed):
    return pl.CostEstimate(flops=flops, bytes_accessed=bytes_accessed, transcendentals=0)


def gradient_kernel(scale, *refs):
    pieces, (saved0, saved1, out) = refs[:8], refs[8:]
    rows = saved0.shape[0]
    left = jnp.concatenate([ref[0] for ref in pieces], axis=1)
    total = jnp.dot(left[:, :rows], saved0[...], preferred_element_type=f32)
    total += jnp.dot(left[:, rows:], saved1[...], preferred_element_type=f32)
    out[...] = (total * scale).astype(bf16)


def gradient_part(pieces, saved0, saved1, index, scale):
    _, own, tok = pieces[0].shape
    rows, wide = saved0.shape
    steps = 2 if own % 32 == 0 else 1
    part = own // steps
    whole = pl.BlockSpec((rows, wide), lambda i: (0, 0))
    return pl.pallas_call(
        functools.partial(gradient_kernel, scale),
        grid=(steps,),
        in_specs=[pl.BlockSpec((1, part, tok), lambda i: (index, i, 0))] * 8 + [whole] * 2,
        out_specs=pl.BlockSpec((part, wide), lambda i: (i, 0)),
        out_shape=jax.ShapeDtypeStruct((own, wide), bf16),
        compiler_params=params(),
        cost_estimate=cost(4 * own * rows * wide, 2 * own * (2 * rows + wide) + 4 * rows * wide),
        name="gradient_part",
    )(*pieces, saved0, saved1)


def attn_kernel(*refs):
    pieces, (weights, kept, sent, total) = refs[:8], refs[8:]
    step = pl.program_id(0)
    rows = kept.shape[0]
    left = jnp.concatenate([ref[0] for ref in pieces], axis=1)
    product = lax.dot_general(left, weights[0], (((0,), (0,)), ((), ())), preferred_element_type=f32)

    @pl.when(step == 0)
    def _():
        total[...] = product

    @pl.when(step > 0)
    def _():
        total[...] += product

    @pl.when(step == pl.num_programs(0) - 1)
    def _():
        kept[...] = total[:rows]
        sent[...] = total[rows:].astype(bf16)


def attn_part(pieces, weights):
    n, own, tok = pieces[0].shape
    wide = weights.shape[2]
    rows = 4 * tok
    whole = pl.BlockSpec((rows, wide), lambda i: (0, 0))
    return pl.pallas_call(
        attn_kernel,
        grid=(n,),
        in_specs=[pl.BlockSpec((1, own, tok), lambda i: (i, 0, 0))] * 8
        + [pl.BlockSpec((1, own, wide), lambda i: (i, 0, 0))],
        out_specs=[whole, whole],
        out_shape=[jax.ShapeDtypeStruct((rows, wide), f32), jax.ShapeDtypeStruct((rows, wide), bf16)],
        scratch_shapes=[pltpu.VMEM((2 * rows, wide), f32)],
        compiler_params=params(),
        cost_estimate=cost(4 * n * own * rows * wide, 2 * n * own * (2 * rows + wide) + 6 * rows * wide),
        name="attn_part",
    )(*pieces, weights)


def outward_kernel(block, next0, next1, kept, sent):
    tok = kept.shape[3]
    for y, following in enumerate((next0, next1)):
        out = lax.dot_general(
            block[...], following[...], (((1,), (1,)), ((), ())), preferred_element_type=f32
        ).astype(bf16)
        for chip in range(2):
            kept[chip, y] = out[:, chip * tok : (chip + 1) * tok]
            sent[chip, y] = out[:, (2 + chip) * tok : (3 + chip) * tok]


def outward_part(block, next0, next1):
    own, wide = block.shape
    rows = next0.shape[0]
    shape = jax.ShapeDtypeStruct((2, 2, own, rows // 4), bf16)
    return pl.pallas_call(
        outward_kernel,
        out_shape=[shape, shape],
        compiler_params=params(),
        cost_estimate=cost(4 * own * rows * wide, 2 * (own * wide + 2 * rows * wide + 2 * own * rows)),
        name="outward_part",
    )(block, next0, next1)


def add(a, b):
    return (a.astype(f32) + b.astype(f32)).astype(bf16)


def local(cotangent, attn_saved, attn_next, weight, moment1, moment2):
    dp, t = lax.axis_index("dp"), lax.axis_index("tensor")
    n = lax.axis_size("dp") // 2
    z, y, x, c = dp // 2, dp % 2, t // 2, t % 2
    own, wide = weight.shape
    tok = cotangent.shape[0]
    scale = 1.0 / math.sqrt(4 * tok * lax.axis_size("dp"))
    order = [n - 1] + [r for r in range(1, n - 1)] + [0]
    top = n // 2
    levels = [[r for r in range(n) if r.bit_count() == k] for k in range(n.bit_length())]
    low, multi = levels[1][:-1], [r for level in levels[2:] for r in level]
    halves = 2 if own % 32 == 0 else 1

    weights = {(0, h): part for h, part in enumerate(jnp.split(weight, halves))}

    def fetch(keys):
        for r, h in keys:
            weights[r, h] = to_plane(weights[r & (r - 1), h], r & -r)

    def hold(keys, *others):
        came, *others = stage([weights[k] for k in keys], *others)
        weights.update(zip(keys, came))
        return others

    second = [(r, 1) for r in range(n)] if halves > 1 else []

    blocks = cotangent.T.reshape(n, 2, own, tok)
    blocks = jnp.take(blocks, z ^ jnp.array(order), axis=0)
    mine = jnp.where(y == 0, blocks[:, 0], blocks[:, 1])
    other = jnp.where(y == 0, blocks[:, 1], blocks[:, 0])
    mine, other = stage(mine, other)
    fetch([(top, 0)] + [(r, 0) for r in low])
    partner = to_partner(other)
    mine_x = to_chip(mine)
    mine_c = to_core(mine)
    saved0 = relative(attn_saved, x, c)
    keys = [(r, 0) for r in levels[1]] + second[:1]
    partner, mine_x, mine_c, saved0 = hold(keys, partner, mine_x, mine_c, saved0)

    saved1 = to_partner(saved0)
    partner_x = to_chip(partner)
    partner_c = to_core(partner)
    mine_xc = to_core(mine_x)
    fetch([k for k in second if k[0] == top])
    keys = [(r, 0) for r in levels[1]] + second[:1]
    partner_c, mine_xc = hold(keys, partner_c, mine_xc)
    fetch([(r, 0) for r in multi] + [k for k in second if k[0] in low])
    keys = [(r, 0) for r in multi] + [k for k in second if k[0] in levels[1]]
    saved1, partner_x = hold(keys, saved1, partner_x)
    partner_xc = to_core(partner_x)
    pieces = [mine, mine_x, mine_c, mine_xc, partner, partner_x, partner_c, partner_xc]

    sums = {}
    for j, r in enumerate(order):
        sums[r] = gradient_part(pieces, saved0, saved1, j, scale)
    next0 = relative(attn_next, x, c)
    next1 = to_partner(next0)
    m = 1
    while m < top:
        sends = [r for r in sums if r & m and r != m]
        came = [to_plane(sums.pop(r), m) for r in sends]
        came, sums[m] = stage(came, sums[m])
        for r, value in zip(sends, came):
            sums[r ^ m] = add(sums[r ^ m], value)
        m *= 2
    ends = [1 << k for k in reversed(range(n.bit_length() - 1))]
    (came,) = hold([k for k in second if k[0] in levels[1]], came)
    fetch([k for k in second if k[0] in multi])
    came = [to_plane(sums[m], m) for m in ends]
    gathered = jnp.stack([jnp.concatenate([weights[r, h] for h in range(halves)]) for r in order])
    kept, sent = attn_part(pieces, gathered)
    sent = to_partner(sent)
    came, kept, sent, next1 = stage(came, kept, sent, next1)
    gradient = sums[0].astype(f32) + functools.reduce(jnp.add, [v.astype(f32) for v in came])
    new_weight, new_moment1, new_moment2 = adamw_step(gradient, weight, moment1, moment2)
    grad_attn = absolute((kept + sent.astype(f32)).astype(bf16), x, c)

    held, results = {0: new_weight}, {}
    for k, wave in enumerate(levels):
        later = levels[k + 1] if k + 1 < len(levels) else []
        for r in reversed(later):
            held[r] = to_plane(held[r & (r - 1)], r & -r)
        kept, came = {}, {}
        for r in wave:
            block, sent = outward_part(held[r], next0, next1)
            half = add(block, to_core(sent))
            kept[r], came[r] = half[0], to_chip(half[1])
        if later:
            blocks, kept = stage([held[r] for r in later], kept)
            blocks, came, results = stage(blocks, came, results)
            held.update(zip(later, blocks))
        for r in wave:
            total = add(kept[r], came[r])
            results[r] = (total[0], to_partner(total[1]))

    mine = jnp.stack([results[r][0] for r in range(n)])
    other = jnp.stack([results[r][1] for r in range(n)])
    both = jnp.stack([jnp.where(y == 0, mine, other), jnp.where(y == 0, other, mine)], axis=1)
    next_out = jnp.take(both, z ^ jnp.arange(n), axis=0).reshape(2 * n * own, tok).T
    return (grad_attn, new_weight, new_moment1, new_moment2, next_out)


def solution(mesh):
    return jax.shard_map(
        local,
        mesh=mesh,
        in_specs=(
            P(("dp", "tensor"), None),
            P("dp", "tensor"),
            P("dp", "tensor"),
            P("dp", "tensor"),
            P("dp", "tensor"),
            P("dp", "tensor"),
        ),
        out_specs=(
            P("dp", "tensor"),
            P("dp", "tensor"),
            P("dp", "tensor"),
            P("dp", "tensor"),
            P(("dp", "tensor"), None),
        ),
        check_vma=False,
    )
```

```python
import functools
import math

import jax
import jax.numpy as jnp
from jax import lax
from jax.experimental import pallas as pl
from jax.experimental.pallas import tpu as pltpu
from jax.sharding import PartitionSpec as P

first_decay = 0.9
second_decay = 0.95
first_fix = 1.0 - 0.9**10
second_fix = 1.0 - 0.95**10
learning_rate = 0.002
weight_decay = 0.1
epsilon = 1e-08
bf16 = jnp.bfloat16
f32 = jnp.float32
VMEM_LIMIT = 48 * 2**20


def adamw_step(gradient, weight, moment1, moment2):
    new_moment1 = first_decay * moment1 + (1.0 - first_decay) * gradient
    new_moment2 = second_decay * moment2 + (1.0 - second_decay) * gradient * gradient
    update = new_moment1 / first_fix / (jnp.sqrt(new_moment2 / second_fix) + epsilon)
    new_weight = (
        weight.astype(f32) * (1.0 - learning_rate * weight_decay) - learning_rate * update
    ).astype(bf16)
    return (new_weight, new_moment1, new_moment2)


def flip(value, axis, bit):
    return lax.ppermute(value, axis, [(i, i ^ bit) for i in range(lax.axis_size(axis))])


def to_partner(value):
    return flip(value, "dp", 1)


def to_chip(value):
    return flip(value, "tensor", 2)


def to_core(value):
    return flip(value, "tensor", 1)


def to_plane(value, bit):
    return flip(value, "dp", 2 * bit)


def stage(*values):
    return lax.optimization_barrier(values)


def relative(rows, x, c):
    block = rows.shape[0] // 4
    rows = rows.reshape(2, 2, block, rows.shape[1])
    rows = jnp.where(x == 1, rows[::-1], rows)
    rows = jnp.where(c == 1, rows[:, ::-1], rows)
    return rows.transpose(1, 0, 2, 3).reshape(4 * block, -1)


def absolute(rows, x, c):
    block = rows.shape[0] // 4
    rows = rows.reshape(2, 2, block, -1).transpose(1, 0, 2, 3)
    rows = jnp.where(c == 1, rows[:, ::-1], rows)
    rows = jnp.where(x == 1, rows[::-1], rows)
    return rows.reshape(4 * block, -1)


def params():
    return pltpu.CompilerParams(vmem_limit_bytes=VMEM_LIMIT)


def cost(flops, bytes_accessed):
    return pl.CostEstimate(flops=flops, bytes_accessed=bytes_accessed, transcendentals=0)


def gradient_kernel(scale, *refs):
    pieces, (saved0, saved1, out) = refs[:8], refs[8:]
    rows = saved0.shape[0]
    left = jnp.concatenate([ref[0] for ref in pieces], axis=1)
    total = jnp.dot(left[:, :rows], saved0[...], preferred_element_type=f32)
    total += jnp.dot(left[:, rows:], saved1[...], preferred_element_type=f32)
    out[...] = (total * scale).astype(bf16)


def gradient_part(pieces, saved0, saved1, index, scale):
    _, own, tok = pieces[0].shape
    rows, wide = saved0.shape
    steps = 2 if own % 32 == 0 else 1
    part = own // steps
    whole = pl.BlockSpec((rows, wide), lambda i: (0, 0))
    return pl.pallas_call(
        functools.partial(gradient_kernel, scale),
        grid=(steps,),
        in_specs=[pl.BlockSpec((1, part, tok), lambda i: (index, i, 0))] * 8 + [whole] * 2,
        out_specs=pl.BlockSpec((part, wide), lambda i: (i, 0)),
        out_shape=jax.ShapeDtypeStruct((own, wide), bf16),
        compiler_params=params(),
        cost_estimate=cost(4 * own * rows * wide, 2 * own * (2 * rows + wide) + 4 * rows * wide),
        name="gradient_part",
    )(*pieces, saved0, saved1)


def attn_kernel(*refs):
    pieces, (weights, kept, sent, total) = refs[:8], refs[8:]
    step = pl.program_id(0)
    rows = kept.shape[0]
    left = jnp.concatenate([ref[0] for ref in pieces], axis=1)
    product = lax.dot_general(left, weights[0], (((0,), (0,)), ((), ())), preferred_element_type=f32)

    @pl.when(step == 0)
    def _():
        total[...] = product

    @pl.when(step > 0)
    def _():
        total[...] += product

    @pl.when(step == pl.num_programs(0) - 1)
    def _():
        kept[...] = total[:rows]
        sent[...] = total[rows:].astype(bf16)


def attn_part(pieces, weights):
    n, own, tok = pieces[0].shape
    wide = weights.shape[2]
    rows = 4 * tok
    whole = pl.BlockSpec((rows, wide), lambda i: (0, 0))
    return pl.pallas_call(
        attn_kernel,
        grid=(n,),
        in_specs=[pl.BlockSpec((1, own, tok), lambda i: (i, 0, 0))] * 8
        + [pl.BlockSpec((1, own, wide), lambda i: (i, 0, 0))],
        out_specs=[whole, whole],
        out_shape=[jax.ShapeDtypeStruct((rows, wide), f32), jax.ShapeDtypeStruct((rows, wide), bf16)],
        scratch_shapes=[pltpu.VMEM((2 * rows, wide), f32)],
        compiler_params=params(),
        cost_estimate=cost(4 * n * own * rows * wide, 2 * n * own * (2 * rows + wide) + 6 * rows * wide),
        name="attn_part",
    )(*pieces, weights)


def outward_kernel(block, next0, next1, kept, sent):
    tok = kept.shape[3]
    for y, following in enumerate((next0, next1)):
        out = lax.dot_general(
            block[...], following[...], (((1,), (1,)), ((), ())), preferred_element_type=f32
        ).astype(bf16)
        for chip in range(2):
            kept[chip, y] = out[:, chip * tok : (chip + 1) * tok]
            sent[chip, y] = out[:, (2 + chip) * tok : (3 + chip) * tok]


def outward_part(block, next0, next1):
    own, wide = block.shape
    rows = next0.shape[0]
    shape = jax.ShapeDtypeStruct((2, 2, own, rows // 4), bf16)
    return pl.pallas_call(
        outward_kernel,
        out_shape=[shape, shape],
        compiler_params=params(),
        cost_estimate=cost(4 * own * rows * wide, 2 * (own * wide + 2 * rows * wide + 2 * own * rows)),
        name="outward_part",
    )(block, next0, next1)


def add(a, b):
    return (a.astype(f32) + b.astype(f32)).astype(bf16)


def local(cotangent, attn_saved, attn_next, weight, moment1, moment2):
    dp, t = lax.axis_index("dp"), lax.axis_index("tensor")
    n = lax.axis_size("dp") // 2
    z, y, x, c = dp // 2, dp % 2, t // 2, t % 2
    own, wide = weight.shape
    tok = cotangent.shape[0]
    scale = 1.0 / math.sqrt(4 * tok * lax.axis_size("dp"))
    order = [n - 1] + [r for r in range(1, n - 1)] + [0]
    top = n // 2
    levels = [[r for r in range(n) if r.bit_count() == k] for k in range(n.bit_length())]

    weights = {0: weight}
    for r in reversed(levels[1]):
        weights[r] = to_plane(weight, r)

    blocks = cotangent.T.reshape(n, 2, own, tok)
    blocks = jnp.take(blocks, z ^ jnp.array(order), axis=0)
    mine = jnp.where(y == 0, blocks[:, 0], blocks[:, 1])
    other = jnp.where(y == 0, blocks[:, 1], blocks[:, 0])
    mine, other = stage(mine, other)
    partner = to_partner(other)
    mine_x = to_chip(mine)
    mine_c = to_core(mine)
    saved0 = relative(attn_saved, x, c)
    partner, mine_x, mine_c, saved0 = stage(partner, mine_x, mine_c, saved0)

    saved1 = to_partner(saved0)
    partner_x = to_chip(partner)
    partner_c = to_core(partner)
    came, saved1, partner_c, mine_x = stage([weights[r] for r in levels[1]], saved1, partner_c, mine_x)
    weights.update(zip(levels[1], came))
    mine_xc = to_core(mine_x)
    partner_x, mine_xc = stage(partner_x, mine_xc)
    for level in levels[2:]:
        for r in level:
            weights[r] = to_plane(weights[r & (r - 1)], r & -r)
    partner_xc = to_core(partner_x)
    pieces = [mine, mine_x, mine_c, mine_xc, partner, partner_x, partner_c, partner_xc]

    sums = {}
    for j, r in enumerate(order):
        sums[r] = gradient_part(pieces, saved0, saved1, j, scale)
    next0 = relative(attn_next, x, c)
    next1 = to_partner(next0)
    m = 1
    while m < top:
        sends = [r for r in sums if r & m and r != m]
        came = [to_plane(sums.pop(r), m) for r in sends]
        came, sums[m] = stage(came, sums[m])
        for r, value in zip(sends, came):
            sums[r ^ m] = add(sums[r ^ m], value)
        m *= 2
    ends = [1 << k for k in reversed(range(n.bit_length() - 1))]
    gathered, _ = stage([weights[r] for r in order], came)
    gathered = jnp.stack(gathered)
    came = [to_plane(sums[m], m) for m in ends]
    kept, sent = attn_part(pieces, gathered)
    came, next1, attn = stage(came, next1, [kept, sent])
    gradient = sums[0].astype(f32) + functools.reduce(jnp.add, [v.astype(f32) for v in came])
    new_weight, new_moment1, new_moment2 = adamw_step(gradient, weight, moment1, moment2)

    held, results = {0: new_weight}, {}
    for k, wave in enumerate(levels):
        later = levels[k + 1] if k + 1 < len(levels) else []
        for r in reversed(later):
            held[r] = to_plane(held[r & (r - 1)], r & -r)
        kept, came = {}, {}
        for r in wave:
            block, sent = outward_part(held[r], next0, next1)
            half = add(block, to_core(sent))
            kept[r], came[r] = half[0], to_chip(half[1])
        if later:
            blocks, kept = stage([held[r] for r in later], kept)
            if k == 0:
                attn = [attn[0], to_partner(attn[1])]
            blocks, came, results, attn = stage(blocks, came, results, attn)
            held.update(zip(later, blocks))
        for r in wave:
            total = add(kept[r], came[r])
            results[r] = (total[0], to_partner(total[1]))

    grad_attn = absolute((attn[0] + attn[1].astype(f32)).astype(bf16), x, c)
    mine = jnp.stack([results[r][0] for r in range(n)])
    other = jnp.stack([results[r][1] for r in range(n)])
    both = jnp.stack([jnp.where(y == 0, mine, other), jnp.where(y == 0, other, mine)], axis=1)
    next_out = jnp.take(both, z ^ jnp.arange(n), axis=0).reshape(2 * n * own, tok).T
    return (grad_attn, new_weight, new_moment1, new_moment2, next_out)


def solution(mesh):
    return jax.shard_map(
        local,
        mesh=mesh,
        in_specs=(
            P(("dp", "tensor"), None),
            P("dp", "tensor"),
            P("dp", "tensor"),
            P("dp", "tensor"),
            P("dp", "tensor"),
            P("dp", "tensor"),
        ),
        out_specs=(
            P("dp", "tensor"),
            P("dp", "tensor"),
            P("dp", "tensor"),
            P("dp", "tensor"),
            P(("dp", "tensor"), None),
        ),
        check_vma=False,
    )
```

```python
import functools
import math

import jax
import jax.numpy as jnp
from jax import lax
from jax.experimental import pallas as pl
from jax.experimental.pallas import tpu as pltpu
from jax.sharding import PartitionSpec as P

first_decay = 0.9
second_decay = 0.95
first_fix = 1.0 - 0.9**10
second_fix = 1.0 - 0.95**10
learning_rate = 0.002
weight_decay = 0.1
epsilon = 1e-08
bf16 = jnp.bfloat16
f32 = jnp.float32
VMEM_LIMIT = 48 * 2**20


def adamw_step(gradient, weight, moment1, moment2):
    new_moment1 = first_decay * moment1 + (1.0 - first_decay) * gradient
    new_moment2 = second_decay * moment2 + (1.0 - second_decay) * gradient * gradient
    update = new_moment1 / first_fix / (jnp.sqrt(new_moment2 / second_fix) + epsilon)
    new_weight = (
        weight.astype(f32) * (1.0 - learning_rate * weight_decay) - learning_rate * update
    ).astype(bf16)
    return (new_weight, new_moment1, new_moment2)


def flip(value, axis, bit):
    return lax.ppermute(value, axis, [(i, i ^ bit) for i in range(lax.axis_size(axis))])


def to_partner(value):
    return flip(value, "dp", 1)


def to_chip(value):
    return flip(value, "tensor", 2)


def to_core(value):
    return flip(value, "tensor", 1)


def to_plane(value, bit):
    return flip(value, "dp", 2 * bit)


def stage(*values):
    return lax.optimization_barrier(values)


def copy_kernel(index, rows, out):
    del index
    out[...] = rows[...]


def reorder(rows, index):
    block, wide = rows.shape[0] // 4, rows.shape[1]
    return pl.pallas_call(
        copy_kernel,
        grid_spec=pltpu.PrefetchScalarGridSpec(
            num_scalar_prefetch=1,
            grid=(4,),
            in_specs=[pl.BlockSpec((block, wide), lambda i, index: (index[i], 0))],
            out_specs=pl.BlockSpec((block, wide), lambda i, index: (i, 0)),
        ),
        out_shape=jax.ShapeDtypeStruct(rows.shape, rows.dtype),
        compiler_params=params(),
        cost_estimate=light(),
        name="reorder",
    )(index, rows)


def split_kernel(starts, cotangent, mine, other, turned):
    n, own, _ = mine.shape
    turned[...] = cotangent[...].T
    for j in range(n):
        mine[j] = turned[pl.ds(pl.multiple_of(starts[j], 16), own)]
        other[j] = turned[pl.ds(pl.multiple_of(starts[n + j], 16), own)]


def split_features(cotangent, own, planes, y):
    tok, features = cotangent.shape
    n = features // (2 * own)
    if own % 16:
        blocks = jnp.take(cotangent.T.reshape(n, 2, own, tok), planes, axis=0)
        mine = jnp.where(y == 0, blocks[:, 0], blocks[:, 1])
        return mine, jnp.where(y == 0, blocks[:, 1], blocks[:, 0])
    starts = jnp.concatenate([(2 * planes + y) * own, (2 * planes + 1 - y) * own]).astype(jnp.int32)
    shape = jax.ShapeDtypeStruct((n, own, tok), bf16)
    return pl.pallas_call(
        split_kernel,
        in_specs=[pl.BlockSpec(memory_space=pltpu.SMEM), pl.BlockSpec(memory_space=pltpu.VMEM)],
        out_shape=[shape, shape],
        scratch_shapes=[pltpu.VMEM((features, tok), bf16)],
        compiler_params=params(),
        cost_estimate=light(),
        name="split_features",
    )(starts, cotangent)


def join_kernel(starts, *refs):
    blocks, out, turned = refs[:-2], refs[-2], refs[-1]
    own = blocks[0].shape[0]
    for j, block in enumerate(blocks):
        turned[pl.ds(pl.multiple_of(starts[j], 16), own)] = block[...]
    out[...] = turned[...].T


def join_features(mine, other, planes, y):
    n, (own, tok) = len(mine), mine[0].shape
    if own % 16:
        mine, other = jnp.stack(mine), jnp.stack(other)
        both = jnp.stack([jnp.where(y == 0, mine, other), jnp.where(y == 0, other, mine)], axis=1)
        place = jnp.zeros(n, jnp.int32).at[planes].set(jnp.arange(n, dtype=jnp.int32))
        return jnp.take(both, place, axis=0).reshape(2 * n * own, tok).T
    starts = jnp.concatenate([(2 * planes + y) * own, (2 * planes + 1 - y) * own]).astype(jnp.int32)
    vmem = pl.BlockSpec(memory_space=pltpu.VMEM)
    return pl.pallas_call(
        join_kernel,
        in_specs=[pl.BlockSpec(memory_space=pltpu.SMEM)] + [vmem] * (2 * n),
        out_shape=jax.ShapeDtypeStruct((tok, 2 * n * own), bf16),
        scratch_shapes=[pltpu.VMEM((2 * n * own, tok), bf16)],
        compiler_params=params(),
        cost_estimate=light(),
        name="join_features",
    )(starts, *mine, *other)


def params():
    return pltpu.CompilerParams(vmem_limit_bytes=VMEM_LIMIT)


def cost(flops, bytes_accessed):
    return pl.CostEstimate(flops=flops, bytes_accessed=bytes_accessed, transcendentals=0)


def light():
    return cost(10**6, 10**5)


def gradient_kernel(scale, *refs):
    pieces, (saved0, saved1, out) = refs[:8], refs[8:]
    rows = saved0.shape[0]
    left = jnp.concatenate([ref[0] for ref in pieces], axis=1)
    total = jnp.dot(left[:, :rows], saved0[...], preferred_element_type=f32)
    total += jnp.dot(left[:, rows:], saved1[...], preferred_element_type=f32)
    out[...] = (total * scale).astype(bf16)


def gradient_part(pieces, saved0, saved1, index, scale):
    _, own, tok = pieces[0].shape
    rows, wide = saved0.shape
    steps = 2 if own % 32 == 0 else 1
    part = own // steps
    whole = pl.BlockSpec((rows, wide), lambda i: (0, 0))
    return pl.pallas_call(
        functools.partial(gradient_kernel, scale),
        grid=(steps,),
        in_specs=[pl.BlockSpec((1, part, tok), lambda i: (index, i, 0))] * 8 + [whole] * 2,
        out_specs=pl.BlockSpec((part, wide), lambda i: (i, 0)),
        out_shape=jax.ShapeDtypeStruct((own, wide), bf16),
        compiler_params=params(),
        cost_estimate=light(),
        name="gradient_part",
    )(*pieces, saved0, saved1)


def attn_kernel(*refs):
    pieces, (weights, kept, sent, total) = refs[:8], refs[8:]
    step = pl.program_id(0)
    rows = kept.shape[0]
    left = jnp.concatenate([ref[0] for ref in pieces], axis=1)
    product = lax.dot_general(left, weights[0], (((0,), (0,)), ((), ())), preferred_element_type=f32)

    @pl.when(step == 0)
    def _():
        total[...] = product

    @pl.when(step > 0)
    def _():
        total[...] += product

    @pl.when(step == pl.num_programs(0) - 1)
    def _():
        kept[...] = total[:rows]
        sent[...] = total[rows:].astype(bf16)


def attn_part(pieces, weights):
    n, own, tok = pieces[0].shape
    wide = weights.shape[2]
    rows = 4 * tok
    whole = pl.BlockSpec((rows, wide), lambda i: (0, 0))
    return pl.pallas_call(
        attn_kernel,
        grid=(n,),
        in_specs=[pl.BlockSpec((1, own, tok), lambda i: (i, 0, 0))] * 8
        + [pl.BlockSpec((1, own, wide), lambda i: (i, 0, 0))],
        out_specs=[whole, whole],
        out_shape=[jax.ShapeDtypeStruct((rows, wide), f32), jax.ShapeDtypeStruct((rows, wide), bf16)],
        scratch_shapes=[pltpu.VMEM((2 * rows, wide), f32)],
        compiler_params=params(),
        cost_estimate=light(),
        name="attn_part",
    )(*pieces, weights)


def outward_kernel(block, next0, next1, kept, sent):
    tok = kept.shape[3]
    for y, following in enumerate((next0, next1)):
        out = lax.dot_general(
            block[...], following[...], (((1,), (1,)), ((), ())), preferred_element_type=f32
        ).astype(bf16)
        for chip in range(2):
            kept[chip, y] = out[:, chip * tok : (chip + 1) * tok]
            sent[chip, y] = out[:, (2 + chip) * tok : (3 + chip) * tok]


def outward_part(block, next0, next1):
    own, wide = block.shape
    rows = next0.shape[0]
    shape = jax.ShapeDtypeStruct((2, 2, own, rows // 4), bf16)
    return pl.pallas_call(
        outward_kernel,
        out_shape=[shape, shape],
        compiler_params=params(),
        cost_estimate=cost(4 * own * rows * wide, 2 * (own * wide + 2 * rows * wide + 2 * own * rows)),
        name="outward_part",
    )(block, next0, next1)


def add(a, b):
    return (a.astype(f32) + b.astype(f32)).astype(bf16)


def local(cotangent, attn_saved, attn_next, weight, moment1, moment2):
    dp, t = lax.axis_index("dp"), lax.axis_index("tensor")
    n = lax.axis_size("dp") // 2
    z, y, x, c = dp // 2, dp % 2, t // 2, t % 2
    own, wide = weight.shape
    tok = cotangent.shape[0]
    scale = 1.0 / math.sqrt(4 * tok * lax.axis_size("dp"))
    order = [n - 1] + [r for r in range(1, n - 1)] + [0]
    top = n // 2
    levels = [[r for r in range(n) if r.bit_count() == k] for k in range(n.bit_length())]

    inward = jnp.stack([2 * (x ^ chip) + (c ^ core) for core in range(2) for chip in range(2)]).astype(jnp.int32)
    back = jnp.stack([2 * (c ^ core) + (x ^ chip) for chip in range(2) for core in range(2)]).astype(jnp.int32)

    weights = {0: weight}
    for r in reversed(levels[1]):
        weights[r] = to_plane(weight, r)

    mine, other = split_features(cotangent, own, z ^ jnp.array(order, jnp.int32), y)
    mine, other = stage(mine, other)
    partner = to_partner(other)
    mine_x = to_chip(mine)
    mine_c = to_core(mine)
    saved0 = reorder(attn_saved, inward)
    partner, mine_x, mine_c, saved0 = stage(partner, mine_x, mine_c, saved0)

    saved1 = to_partner(saved0)
    partner_x = to_chip(partner)
    partner_c = to_core(partner)
    came, saved1, partner_c, mine_x = stage([weights[r] for r in levels[1]], saved1, partner_c, mine_x)
    weights.update(zip(levels[1], came))
    mine_xc = to_core(mine_x)
    partner_x, mine_xc = stage(partner_x, mine_xc)
    for level in levels[2:]:
        for r in level:
            weights[r] = to_plane(weights[r & (r - 1)], r & -r)
    partner_xc = to_core(partner_x)
    pieces = [mine, mine_x, mine_c, mine_xc, partner, partner_x, partner_c, partner_xc]

    sums = {}
    for j, r in enumerate(order):
        sums[r] = gradient_part(pieces, saved0, saved1, j, scale)
    next0 = reorder(attn_next, inward)
    next1 = to_partner(next0)
    m = 1
    while m < top:
        sends = [r for r in sums if r & m and r != m]
        came = [to_plane(sums.pop(r), m) for r in sends]
        last = [r for r in order if r.bit_count() > 1]
        old, came, sums[m] = stage([weights[r] for r in last], came, sums[m])
        weights.update(zip(last, old))
        for r, value in zip(sends, came):
            sums[r ^ m] = add(sums[r ^ m], value)
        m *= 2
    ends = [1 << k for k in reversed(range(n.bit_length() - 1))]
    gathered, _ = stage([weights[r] for r in order], came)
    gathered = jnp.stack(gathered)
    came = [to_plane(value, m) for m, value in zip(ends, stage(*[sums[m] for m in ends]))]
    kept, sent = attn_part(pieces, gathered)
    came, next1, attn = stage(came, next1, [kept, sent])
    gradient = sums[0].astype(f32) + functools.reduce(jnp.add, [v.astype(f32) for v in came])
    new_weight, new_moment1, new_moment2 = adamw_step(gradient, weight, moment1, moment2)

    held, results = {0: new_weight}, {}
    for k, wave in enumerate(levels):
        later = levels[k + 1] if k + 1 < len(levels) else []
        for r in reversed(later):
            held[r] = to_plane(held[r & (r - 1)], r & -r)
        kept, came = {}, {}
        for r in wave:
            block, sent = outward_part(held[r], next0, next1)
            half = add(block, to_core(sent))
            kept[r], came[r] = half[0], to_chip(half[1])
        if later:
            blocks, kept = stage([held[r] for r in later], kept)
            if k == 0:
                attn = [attn[0], to_partner(attn[1])]
            blocks, came, results, attn = stage(blocks, came, results, attn)
            held.update(zip(later, blocks))
        for r in wave:
            total = add(kept[r], came[r])
            results[r] = (total[0], to_partner(total[1]))

    grad_attn = reorder((attn[0] + attn[1].astype(f32)).astype(bf16), back)
    mine, other = [[results[r][k] for r in range(n)] for k in range(2)]
    next_out = join_features(mine, other, z ^ jnp.arange(n, dtype=jnp.int32), y)
    return (grad_attn, new_weight, new_moment1, new_moment2, next_out)


def solution(mesh):
    return jax.shard_map(
        local,
        mesh=mesh,
        in_specs=(
            P(("dp", "tensor"), None),
            P("dp", "tensor"),
            P("dp", "tensor"),
            P("dp", "tensor"),
            P("dp", "tensor"),
            P("dp", "tensor"),
        ),
        out_specs=(
            P("dp", "tensor"),
            P("dp", "tensor"),
            P("dp", "tensor"),
            P("dp", "tensor"),
            P(("dp", "tensor"), None),
        ),
        check_vma=False,
    )
```

```python
import functools
import math

import jax
import jax.numpy as jnp
from jax import lax
from jax.experimental import pallas as pl
from jax.experimental.pallas import tpu as pltpu
from jax.sharding import PartitionSpec as P

first_decay = 0.9
second_decay = 0.95
first_fix = 1.0 - 0.9**10
second_fix = 1.0 - 0.95**10
learning_rate = 0.002
weight_decay = 0.1
epsilon = 1e-08
bf16 = jnp.bfloat16
f32 = jnp.float32
VMEM_LIMIT = 48 * 2**20


def adamw_step(gradient, weight, moment1, moment2):
    new_moment1 = first_decay * moment1 + (1.0 - first_decay) * gradient
    new_moment2 = second_decay * moment2 + (1.0 - second_decay) * gradient * gradient
    update = new_moment1 / first_fix / (jnp.sqrt(new_moment2 / second_fix) + epsilon)
    new_weight = (
        weight.astype(f32) * (1.0 - learning_rate * weight_decay) - learning_rate * update
    ).astype(bf16)
    return (new_weight, new_moment1, new_moment2)


def flip(value, axis, bit):
    return lax.ppermute(value, axis, [(i, i ^ bit) for i in range(lax.axis_size(axis))])


def to_partner(value):
    return flip(value, "dp", 1)


def to_chip(value):
    return flip(value, "tensor", 2)


def to_core(value):
    return flip(value, "tensor", 1)


def to_plane(value, bit):
    return flip(value, "dp", 2 * bit)


def stage(*values):
    return lax.optimization_barrier(values)


def copy_kernel(index, rows, out):
    del index
    out[...] = rows[...]


def reorder(rows, index):
    block, wide = rows.shape[0] // 4, rows.shape[1]
    return pl.pallas_call(
        copy_kernel,
        grid_spec=pltpu.PrefetchScalarGridSpec(
            num_scalar_prefetch=1,
            grid=(4,),
            in_specs=[pl.BlockSpec((block, wide), lambda i, index: (index[i], 0))],
            out_specs=pl.BlockSpec((block, wide), lambda i, index: (i, 0)),
        ),
        out_shape=jax.ShapeDtypeStruct(rows.shape, rows.dtype),
        compiler_params=params(),
        cost_estimate=light(),
        name="reorder",
    )(index, rows)


def split_kernel(starts, cotangent, mine, other, turned):
    n, own, _ = mine.shape
    turned[...] = cotangent[...].T
    for j in range(n):
        mine[j] = turned[pl.ds(pl.multiple_of(starts[j], 16), own)]
        other[j] = turned[pl.ds(pl.multiple_of(starts[n + j], 16), own)]


def split_features(cotangent, own, planes, y):
    tok, features = cotangent.shape
    n = features // (2 * own)
    if own % 16:
        blocks = jnp.take(cotangent.T.reshape(n, 2, own, tok), planes, axis=0)
        mine = jnp.where(y == 0, blocks[:, 0], blocks[:, 1])
        return mine, jnp.where(y == 0, blocks[:, 1], blocks[:, 0])
    starts = jnp.concatenate([(2 * planes + y) * own, (2 * planes + 1 - y) * own]).astype(jnp.int32)
    shape = jax.ShapeDtypeStruct((n, own, tok), bf16)
    return pl.pallas_call(
        split_kernel,
        in_specs=[pl.BlockSpec(memory_space=pltpu.SMEM), pl.BlockSpec(memory_space=pltpu.VMEM)],
        out_shape=[shape, shape],
        scratch_shapes=[pltpu.VMEM((features, tok), bf16)],
        compiler_params=params(),
        cost_estimate=light(),
        name="split_features",
    )(starts, cotangent)


def join_kernel(cuts, starts, *refs):
    blocks, out, turned = refs[:-2], refs[-2], refs[-1]
    for j, (block, first, rows) in enumerate(cuts):
        turned[pl.ds(pl.multiple_of(starts[j], 16), rows)] = blocks[block][first : first + rows]
    out[...] = turned[...].T


def join_features(mine, other, cuts, planes, offsets, y):
    n, (own, tok) = len(mine), mine[0].shape
    if own % 16:
        mine, other = jnp.stack(mine), jnp.stack(other)
        both = jnp.stack([jnp.where(y == 0, mine, other), jnp.where(y == 0, other, mine)], axis=1)
        place = jnp.zeros(n, jnp.int32).at[planes].set(jnp.arange(n, dtype=jnp.int32))
        return jnp.take(both, place, axis=0).reshape(2 * n * own, tok).T
    offsets = jnp.array(offsets, jnp.int32)
    starts = [(2 * planes + parity) * own + offsets for parity in (y, 1 - y)]
    cuts = cuts + [(n + block, first, rows) for block, first, rows in cuts]
    vmem = pl.BlockSpec(memory_space=pltpu.VMEM)
    return pl.pallas_call(
        functools.partial(join_kernel, cuts),
        in_specs=[pl.BlockSpec(memory_space=pltpu.SMEM)] + [vmem] * (2 * n),
        out_shape=jax.ShapeDtypeStruct((tok, 2 * n * own), bf16),
        scratch_shapes=[pltpu.VMEM((2 * n * own, tok), bf16)],
        compiler_params=params(),
        cost_estimate=light(),
        name="join_features",
    )(jnp.concatenate(starts).astype(jnp.int32), *mine, *other)


def params():
    return pltpu.CompilerParams(vmem_limit_bytes=VMEM_LIMIT)


def cost(flops, bytes_accessed):
    return pl.CostEstimate(flops=flops, bytes_accessed=bytes_accessed, transcendentals=0)


def light():
    return cost(10**6, 10**5)


def gradient_kernel(scale, *refs):
    pieces, (saved0, saved1, out) = refs[:8], refs[8:]
    rows = saved0.shape[0]
    left = jnp.concatenate([ref[0] for ref in pieces], axis=1)
    total = jnp.dot(left[:, :rows], saved0[...], preferred_element_type=f32)
    total += jnp.dot(left[:, rows:], saved1[...], preferred_element_type=f32)
    out[...] = (total * scale).astype(bf16)


def gradient_part(pieces, saved0, saved1, index, scale):
    _, own, tok = pieces[0].shape
    rows, wide = saved0.shape
    steps = 2 if own % 32 == 0 else 1
    part = own // steps
    whole = pl.BlockSpec((rows, wide), lambda i: (0, 0))
    return pl.pallas_call(
        functools.partial(gradient_kernel, scale),
        grid=(steps,),
        in_specs=[pl.BlockSpec((1, part, tok), lambda i: (index, i, 0))] * 8 + [whole] * 2,
        out_specs=pl.BlockSpec((part, wide), lambda i: (i, 0)),
        out_shape=jax.ShapeDtypeStruct((own, wide), bf16),
        compiler_params=params(),
        cost_estimate=light(),
        name="gradient_part",
    )(*pieces, saved0, saved1)


def attn_kernel(*refs):
    pieces, (weights, kept, sent, total) = refs[:8], refs[8:]
    step = pl.program_id(0)
    rows = kept.shape[0]
    left = jnp.concatenate([ref[0] for ref in pieces], axis=1)
    product = lax.dot_general(left, weights[0], (((0,), (0,)), ((), ())), preferred_element_type=f32)

    @pl.when(step == 0)
    def _():
        total[...] = product

    @pl.when(step > 0)
    def _():
        total[...] += product

    @pl.when(step == pl.num_programs(0) - 1)
    def _():
        kept[...] = total[:rows]
        sent[...] = total[rows:].astype(bf16)


def attn_part(pieces, weights):
    n, own, tok = pieces[0].shape
    wide = weights.shape[2]
    rows = 4 * tok
    whole = pl.BlockSpec((rows, wide), lambda i: (0, 0))
    return pl.pallas_call(
        attn_kernel,
        grid=(n,),
        in_specs=[pl.BlockSpec((1, own, tok), lambda i: (i, 0, 0))] * 8
        + [pl.BlockSpec((1, own, wide), lambda i: (i, 0, 0))],
        out_specs=[whole, whole],
        out_shape=[jax.ShapeDtypeStruct((rows, wide), f32), jax.ShapeDtypeStruct((rows, wide), bf16)],
        scratch_shapes=[pltpu.VMEM((2 * rows, wide), f32)],
        compiler_params=params(),
        cost_estimate=light(),
        name="attn_part",
    )(*pieces, weights)


def outward_kernel(block, next0, next1, kept, sent):
    tok = kept.shape[3]
    for y, following in enumerate((next0, next1)):
        out = lax.dot_general(
            block[...], following[...], (((1,), (1,)), ((), ())), preferred_element_type=f32
        ).astype(bf16)
        for chip in range(2):
            kept[chip, y] = out[:, chip * tok : (chip + 1) * tok]
            sent[chip, y] = out[:, (2 + chip) * tok : (3 + chip) * tok]


def outward_part(block, next0, next1):
    own, wide = block.shape
    rows = next0.shape[0]
    shape = jax.ShapeDtypeStruct((2, 2, own, rows // 4), bf16)
    return pl.pallas_call(
        outward_kernel,
        out_shape=[shape, shape],
        compiler_params=params(),
        cost_estimate=cost(4 * own * rows * wide, 2 * (own * wide + 2 * rows * wide + 2 * own * rows)),
        name="outward_part",
    )(block, next0, next1)


def add(a, b):
    return (a.astype(f32) + b.astype(f32)).astype(bf16)


def local(cotangent, attn_saved, attn_next, weight, moment1, moment2):
    dp, t = lax.axis_index("dp"), lax.axis_index("tensor")
    n = lax.axis_size("dp") // 2
    z, y, x, c = dp // 2, dp % 2, t // 2, t % 2
    own, wide = weight.shape
    tok = cotangent.shape[0]
    scale = 1.0 / math.sqrt(4 * tok * lax.axis_size("dp"))
    order = [n - 1] + [r for r in range(1, n - 1)] + [0]
    top = n // 2
    levels = [[r for r in range(n) if r.bit_count() == k] for k in range(n.bit_length())]

    inward = jnp.stack([2 * (x ^ chip) + (c ^ core) for core in range(2) for chip in range(2)]).astype(jnp.int32)
    back = jnp.stack([2 * (c ^ core) + (x ^ chip) for chip in range(2) for core in range(2)]).astype(jnp.int32)

    weights = {0: weight}
    for r in reversed(levels[1]):
        weights[r] = to_plane(weight, r)

    mine, other = split_features(cotangent, own, z ^ jnp.array(order, jnp.int32), y)
    mine, other = stage(mine, other)
    partner = to_partner(other)
    mine_x = to_chip(mine)
    mine_c = to_core(mine)
    saved0 = reorder(attn_saved, inward)
    partner, mine_x, mine_c, saved0 = stage(partner, mine_x, mine_c, saved0)

    saved1 = to_partner(saved0)
    partner_x = to_chip(partner)
    partner_c = to_core(partner)
    came, saved1, partner_c, mine_x = stage([weights[r] for r in levels[1]], saved1, partner_c, mine_x)
    weights.update(zip(levels[1], came))
    mine_xc = to_core(mine_x)
    partner_x, mine_xc = stage(partner_x, mine_xc)
    for level in levels[2:]:
        for r in level:
            weights[r] = to_plane(weights[r & (r - 1)], r & -r)
    partner_xc = to_core(partner_x)
    pieces = [mine, mine_x, mine_c, mine_xc, partner, partner_x, partner_c, partner_xc]

    sums = {}
    for j, r in enumerate(order):
        sums[r] = gradient_part(pieces, saved0, saved1, j, scale)
    last = [r for r in order if r.bit_count() > 1]
    halved = n == 4 and own % 32 == 0
    cut = own // 2
    if halved:
        far = sums.pop(3)
        came = to_plane(far[:cut], 1)
        old, came, far, near = stage([weights[r] for r in last], came, far, sums[1])
        weights.update(zip(last, old))
        came_a = to_plane(add(sums[2][:cut], came), 2)
        came_b = to_plane(far[cut:], 1)
        came_a, came_b, near = stage(came_a, came_b, near)
        came_b = to_plane(add(sums[2][cut:], came_b), 2)
        came = [came_b, to_plane(near, 1)]
    else:
        m = 1
        while m < top:
            sends = [r for r in sums if r & m and r != m]
            came = [to_plane(sums.pop(r), m) for r in sends]
            old, came, sums[m] = stage([weights[r] for r in last], came, sums[m])
            weights.update(zip(last, old))
            for r, value in zip(sends, came):
                sums[r ^ m] = add(sums[r ^ m], value)
            m *= 2
        ends = [1 << k for k in reversed(range(n.bit_length() - 1))]
        came = [to_plane(value, m) for m, value in zip(ends, stage(*[sums[m] for m in ends]))]
    next0 = reorder(attn_next, inward)
    next1 = to_partner(next0)
    kept, sent = attn_part(pieces, jnp.stack([weights[r] for r in order]))
    came, next1, attn = stage(came, next1, [kept, sent])
    if halved:
        came[0] = jnp.concatenate([came_a, came[0]])
    gradient = sums[0].astype(f32) + functools.reduce(jnp.add, [v.astype(f32) for v in came])
    new_weight, new_moment1, new_moment2 = adamw_step(gradient, weight, moment1, moment2)

    def outward(block):
        own_core, other_core = outward_part(block, next0, next1)
        half = add(own_core, to_core(other_core))
        return half[0], to_chip(half[1])

    def finish(kept, came):
        total = add(kept, came)
        return total[0], to_partner(total[1])

    if halved:
        near = to_plane(new_weight, 1)
        far_a = to_plane(new_weight[:cut], 2)
        kept0, came0 = outward(new_weight)
        near, far_a, kept0 = stage(near, far_a, kept0)
        near, far_a, came0, rest, attn = stage(near, far_a, came0, new_weight, attn)
        far_b = to_plane(rest[cut:], 2)
        both_a = to_plane(far_a, 1)
        attn = [attn[0], to_partner(attn[1])]
        kept1, came1 = outward(near)
        far_b, both_a, kept1 = stage(far_b, both_a, kept1)
        far_b, both_a, came1, attn = stage(far_b, both_a, came1, attn)
        both_b = to_plane(far_b, 1)
        result0 = finish(kept0, came0)
        kept2, came2 = outward(jnp.concatenate([far_a, both_a]))
        both_b, kept2 = stage(both_b, kept2)
        both_b, came2, result0 = stage(both_b, came2, result0)
        result1, result2 = finish(kept1, came1), finish(kept2, came2)
        results = [result0, result1, result2, finish(*outward(jnp.concatenate([far_b, both_b])))]
        cuts = [(0, 0, own), (1, 0, own), (2, 0, cut), (2, cut, cut), (3, 0, cut), (3, cut, cut)]
        offsets = [0, 0, 0, 0, cut, cut]
        planes = z ^ jnp.array([0, 1, 2, 3, 2, 3], jnp.int32)
    else:
        held, results = {0: new_weight}, {}
        for k, wave in enumerate(levels):
            later = levels[k + 1] if k + 1 < len(levels) else []
            for r in reversed(later):
                held[r] = to_plane(held[r & (r - 1)], r & -r)
            kept, came = {}, {}
            for r in wave:
                kept[r], came[r] = outward(held[r])
            if later:
                blocks, kept = stage([held[r] for r in later], kept)
                if k == 0:
                    attn = [attn[0], to_partner(attn[1])]
                blocks, came, results, attn = stage(blocks, came, results, attn)
                held.update(zip(later, blocks))
            for r in wave:
                results[r] = finish(kept[r], came[r])
        results = [results[r] for r in range(n)]
        cuts, offsets = [(r, 0, own) for r in range(n)], [0] * n
        planes = z ^ jnp.arange(n, dtype=jnp.int32)

    grad_attn = reorder((attn[0] + attn[1].astype(f32)).astype(bf16), back)
    mine, other = [[result[k] for result in results] for k in range(2)]
    next_out = join_features(mine, other, cuts, planes, offsets, y)
    return (grad_attn, new_weight, new_moment1, new_moment2, next_out)


def solution(mesh):
    return jax.shard_map(
        local,
        mesh=mesh,
        in_specs=(
            P(("dp", "tensor"), None),
            P("dp", "tensor"),
            P("dp", "tensor"),
            P("dp", "tensor"),
            P("dp", "tensor"),
            P("dp", "tensor"),
        ),
        out_specs=(
            P("dp", "tensor"),
            P("dp", "tensor"),
            P("dp", "tensor"),
            P("dp", "tensor"),
            P(("dp", "tensor"), None),
        ),
        check_vma=False,
    )
```

```python
import functools
import math

import jax
import jax.numpy as jnp
from jax import lax
from jax.experimental import pallas as pl
from jax.experimental.pallas import tpu as pltpu
from jax.sharding import PartitionSpec as P

first_decay = 0.9
second_decay = 0.95
first_fix = 1.0 - 0.9**10
second_fix = 1.0 - 0.95**10
learning_rate = 0.002
weight_decay = 0.1
epsilon = 1e-08
bf16 = jnp.bfloat16
f32 = jnp.float32


def adamw_step(gradient, weight, moment1, moment2):
    new_moment1 = first_decay * moment1 + (1.0 - first_decay) * gradient
    new_moment2 = second_decay * moment2 + (1.0 - second_decay) * gradient * gradient
    update = new_moment1 / first_fix / (jnp.sqrt(new_moment2 / second_fix) + epsilon)
    new_weight = (
        weight.astype(f32) * (1.0 - learning_rate * weight_decay) - learning_rate * update
    ).astype(bf16)
    return (new_weight, new_moment1, new_moment2)


def flip(value, axis, bit):
    return lax.ppermute(value, axis, [(i, i ^ bit) for i in range(lax.axis_size(axis))])


def to_partner(value):
    return flip(value, "dp", 1)


def to_chip(value):
    return flip(value, "tensor", 2)


def to_core(value):
    return flip(value, "tensor", 1)


def to_plane(value, bit):
    return flip(value, "dp", 2 * bit)


def stage(*values):
    return lax.optimization_barrier(values)


def copy_kernel(index, rows, out):
    del index
    out[...] = rows[...]


def reorder(rows, index):
    block, wide = rows.shape[0] // 4, rows.shape[1]
    return pl.pallas_call(
        copy_kernel,
        grid_spec=pltpu.PrefetchScalarGridSpec(
            num_scalar_prefetch=1,
            grid=(4,),
            in_specs=[pl.BlockSpec((block, wide), lambda i, index: (index[i], 0))],
            out_specs=pl.BlockSpec((block, wide), lambda i, index: (i, 0)),
        ),
        out_shape=jax.ShapeDtypeStruct(rows.shape, rows.dtype),
        compiler_params=params(4),
        cost_estimate=light(),
        name="reorder",
    )(index, rows)


def split_kernel(starts, cotangent, mine, other, turned):
    n, own, _ = mine.shape
    turned[...] = cotangent[...].T
    for j in range(n):
        mine[j] = turned[pl.ds(pl.multiple_of(starts[j], 16), own)]
        other[j] = turned[pl.ds(pl.multiple_of(starts[n + j], 16), own)]


def split_features(cotangent, own, planes, y):
    tok, features = cotangent.shape
    n = features // (2 * own)
    if own % 16:
        blocks = jnp.take(cotangent.T.reshape(n, 2, own, tok), planes, axis=0)
        mine = jnp.where(y == 0, blocks[:, 0], blocks[:, 1])
        return mine, jnp.where(y == 0, blocks[:, 1], blocks[:, 0])
    starts = jnp.concatenate([(2 * planes + y) * own, (2 * planes + 1 - y) * own]).astype(jnp.int32)
    shape = jax.ShapeDtypeStruct((n, own, tok), bf16)
    return pl.pallas_call(
        split_kernel,
        in_specs=[pl.BlockSpec(memory_space=pltpu.SMEM), pl.BlockSpec(memory_space=pltpu.VMEM)],
        out_shape=[shape, shape],
        scratch_shapes=[pltpu.VMEM((features, tok), bf16)],
        compiler_params=params(12),
        cost_estimate=light(),
        name="split_features",
    )(starts, cotangent)


def join_kernel(starts, *refs):
    blocks, out, turned = refs[:-2], refs[-2], refs[-1]
    own = blocks[0].shape[0]
    for j, block in enumerate(blocks):
        turned[pl.ds(pl.multiple_of(starts[j], 16), own)] = block[...]
    out[...] = turned[...].T


def join_features(mine, other, planes, y):
    n, (own, tok) = len(mine), mine[0].shape
    if own % 16:
        mine, other = jnp.stack(mine), jnp.stack(other)
        both = jnp.stack([jnp.where(y == 0, mine, other), jnp.where(y == 0, other, mine)], axis=1)
        place = jnp.zeros(n, jnp.int32).at[planes].set(jnp.arange(n, dtype=jnp.int32))
        return jnp.take(both, place, axis=0).reshape(2 * n * own, tok).T
    starts = jnp.concatenate([(2 * planes + y) * own, (2 * planes + 1 - y) * own]).astype(jnp.int32)
    vmem = pl.BlockSpec(memory_space=pltpu.VMEM)
    return pl.pallas_call(
        join_kernel,
        in_specs=[pl.BlockSpec(memory_space=pltpu.SMEM)] + [vmem] * (2 * n),
        out_shape=jax.ShapeDtypeStruct((tok, 2 * n * own), bf16),
        scratch_shapes=[pltpu.VMEM((2 * n * own, tok), bf16)],
        compiler_params=params(12),
        cost_estimate=light(),
        name="join_features",
    )(starts, *mine, *other)


def params(mib):
    return pltpu.CompilerParams(vmem_limit_bytes=mib * 2**20)


def cost(flops, bytes_accessed):
    return pl.CostEstimate(flops=flops, bytes_accessed=bytes_accessed, transcendentals=0)


def light():
    return cost(10**6, 10**5)


def gradient_kernel(scale, *refs):
    pieces, (saved0, saved1, out) = refs[:8], refs[8:]
    rows = saved0.shape[0]
    left = jnp.concatenate([ref[0] for ref in pieces], axis=1)
    total = jnp.dot(left[:, :rows], saved0[...], preferred_element_type=f32)
    total += jnp.dot(left[:, rows:], saved1[...], preferred_element_type=f32)
    out[...] = (total * scale).astype(bf16)


def gradient_part(pieces, saved0, saved1, index, scale):
    _, own, tok = pieces[0].shape
    rows, wide = saved0.shape
    steps = 2 if own % 32 == 0 else 1
    part = own // steps
    whole = pl.BlockSpec((rows, wide), lambda i: (0, 0))
    return pl.pallas_call(
        functools.partial(gradient_kernel, scale),
        grid=(steps,),
        in_specs=[pl.BlockSpec((1, part, tok), lambda i: (index, i, 0))] * 8 + [whole] * 2,
        out_specs=pl.BlockSpec((part, wide), lambda i: (i, 0)),
        out_shape=jax.ShapeDtypeStruct((own, wide), bf16),
        compiler_params=params(12),
        cost_estimate=light(),
        name="gradient_part",
    )(*pieces, saved0, saved1)


def attn_kernel(*refs):
    pieces, (weights, kept, sent, total) = refs[:8], refs[8:]
    step = pl.program_id(0)
    rows = kept.shape[0]
    left = jnp.concatenate([ref[0] for ref in pieces], axis=1)
    product = lax.dot_general(left, weights[0], (((0,), (0,)), ((), ())), preferred_element_type=f32)

    @pl.when(step == 0)
    def _():
        total[...] = product

    @pl.when(step > 0)
    def _():
        total[...] += product

    @pl.when(step == pl.num_programs(0) - 1)
    def _():
        kept[...] = total[:rows]
        sent[...] = total[rows:].astype(bf16)


def attn_part(pieces, weights):
    n, own, tok = pieces[0].shape
    wide = weights.shape[2]
    rows = 4 * tok
    whole = pl.BlockSpec((rows, wide), lambda i: (0, 0))
    return pl.pallas_call(
        attn_kernel,
        grid=(n,),
        in_specs=[pl.BlockSpec((1, own, tok), lambda i: (i, 0, 0))] * 8
        + [pl.BlockSpec((1, own, wide), lambda i: (i, 0, 0))],
        out_specs=[whole, whole],
        out_shape=[jax.ShapeDtypeStruct((rows, wide), f32), jax.ShapeDtypeStruct((rows, wide), bf16)],
        scratch_shapes=[pltpu.VMEM((2 * rows, wide), f32)],
        compiler_params=params(24),
        cost_estimate=light(),
        name="attn_part",
    )(*pieces, weights)


def outward_kernel(block, next0, next1, kept, sent):
    tok = kept.shape[3]
    for y, following in enumerate((next0, next1)):
        out = lax.dot_general(
            block[...], following[...], (((1,), (1,)), ((), ())), preferred_element_type=f32
        ).astype(bf16)
        for chip in range(2):
            kept[chip, y] = out[:, chip * tok : (chip + 1) * tok]
            sent[chip, y] = out[:, (2 + chip) * tok : (3 + chip) * tok]


def outward_part(block, next0, next1):
    own, wide = block.shape
    rows = next0.shape[0]
    shape = jax.ShapeDtypeStruct((2, 2, own, rows // 4), bf16)
    return pl.pallas_call(
        outward_kernel,
        out_shape=[shape, shape],
        compiler_params=params(12),
        cost_estimate=cost(4 * own * rows * wide, 2 * (own * wide + 2 * rows * wide + 2 * own * rows)),
        name="outward_part",
    )(block, next0, next1)


def add(a, b):
    return (a.astype(f32) + b.astype(f32)).astype(bf16)


def local(cotangent, attn_saved, attn_next, weight, moment1, moment2):
    dp, t = lax.axis_index("dp"), lax.axis_index("tensor")
    n = lax.axis_size("dp") // 2
    z, y, x, c = dp // 2, dp % 2, t // 2, t % 2
    own, wide = weight.shape
    tok = cotangent.shape[0]
    scale = 1.0 / math.sqrt(4 * tok * lax.axis_size("dp"))
    order = [n - 1] + [r for r in range(1, n - 1)] + [0]
    top = n // 2
    levels = [[r for r in range(n) if r.bit_count() == k] for k in range(n.bit_length())]

    inward = jnp.stack([2 * (x ^ chip) + (c ^ core) for core in range(2) for chip in range(2)]).astype(jnp.int32)
    back = jnp.stack([2 * (c ^ core) + (x ^ chip) for chip in range(2) for core in range(2)]).astype(jnp.int32)

    weights = {0: weight}
    for r in reversed(levels[1]):
        weights[r] = to_plane(weight, r)

    mine, other = split_features(cotangent, own, z ^ jnp.array(order, jnp.int32), y)
    mine, other = stage(mine, other)
    partner = to_partner(other)
    mine_x = to_chip(mine)
    mine_c = to_core(mine)
    saved0 = reorder(attn_saved, inward)
    partner, mine_x, mine_c, saved0 = stage(partner, mine_x, mine_c, saved0)

    saved1 = to_partner(saved0)
    partner_x = to_chip(partner)
    partner_c = to_core(partner)
    came, saved1, partner_c, mine_x = stage([weights[r] for r in levels[1]], saved1, partner_c, mine_x)
    weights.update(zip(levels[1], came))
    mine_xc = to_core(mine_x)
    partner_x, mine_xc = stage(partner_x, mine_xc)
    for level in levels[2:]:
        for r in level:
            weights[r] = to_plane(weights[r & (r - 1)], r & -r)
    partner_xc = to_core(partner_x)
    pieces = [mine, mine_x, mine_c, mine_xc, partner, partner_x, partner_c, partner_xc]

    sums = {}
    for j, r in enumerate(order):
        sums[r] = gradient_part(pieces, saved0, saved1, j, scale)
    next0 = reorder(attn_next, inward)
    next1 = to_partner(next0)
    m = 1
    while m < top:
        sends = [r for r in sums if r & m and r != m]
        came = [to_plane(sums.pop(r), m) for r in sends]
        last = [r for r in order if r.bit_count() > 1]
        old, came, sums[m] = stage([weights[r] for r in last], came, sums[m])
        weights.update(zip(last, old))
        for r, value in zip(sends, came):
            sums[r ^ m] = add(sums[r ^ m], value)
        m *= 2
    ends = [1 << k for k in reversed(range(n.bit_length() - 1))]
    gathered, _ = stage([weights[r] for r in order], came)
    gathered = jnp.stack(gathered)
    came = [to_plane(value, m) for m, value in zip(ends, stage(*[sums[m] for m in ends]))]
    kept, sent = attn_part(pieces, gathered)
    came, next1, attn = stage(came, next1, [kept, sent])
    gradient = sums[0].astype(f32) + functools.reduce(jnp.add, [v.astype(f32) for v in came])
    new_weight, new_moment1, new_moment2 = adamw_step(gradient, weight, moment1, moment2)

    held, results = {0: new_weight}, {}
    for k, wave in enumerate(levels):
        later = levels[k + 1] if k + 1 < len(levels) else []
        for r in reversed(later):
            held[r] = to_plane(held[r & (r - 1)], r & -r)
        kept, came = {}, {}
        for r in wave:
            block, sent = outward_part(held[r], next0, next1)
            half = add(block, to_core(sent))
            kept[r], came[r] = half[0], to_chip(half[1])
        if later:
            blocks, kept = stage([held[r] for r in later], kept)
            if k == 0:
                attn = [attn[0], to_partner(attn[1])]
            blocks, came, results, attn = stage(blocks, came, results, attn)
            held.update(zip(later, blocks))
        for r in wave:
            total = add(kept[r], came[r])
            results[r] = (total[0], to_partner(total[1]))

    grad_attn = reorder((attn[0] + attn[1].astype(f32)).astype(bf16), back)
    mine, other = [[results[r][k] for r in range(n)] for k in range(2)]
    next_out = join_features(mine, other, z ^ jnp.arange(n, dtype=jnp.int32), y)
    return (grad_attn, new_weight, new_moment1, new_moment2, next_out)


def solution(mesh):
    return jax.shard_map(
        local,
        mesh=mesh,
        in_specs=(
            P(("dp", "tensor"), None),
            P("dp", "tensor"),
            P("dp", "tensor"),
            P("dp", "tensor"),
            P("dp", "tensor"),
            P("dp", "tensor"),
        ),
        out_specs=(
            P("dp", "tensor"),
            P("dp", "tensor"),
            P("dp", "tensor"),
            P("dp", "tensor"),
            P(("dp", "tensor"), None),
        ),
        check_vma=False,
    )
```

```python
import functools
import math

import jax
import jax.numpy as jnp
from jax import lax
from jax.experimental import pallas as pl
from jax.experimental.pallas import tpu as pltpu
from jax.sharding import PartitionSpec as P

first_decay = 0.9
second_decay = 0.95
first_fix = 1.0 - 0.9**10
second_fix = 1.0 - 0.95**10
learning_rate = 0.002
weight_decay = 0.1
epsilon = 1e-08
bf16 = jnp.bfloat16
f32 = jnp.float32


def adamw_step(gradient, weight, moment1, moment2):
    new_moment1 = first_decay * moment1 + (1.0 - first_decay) * gradient
    new_moment2 = second_decay * moment2 + (1.0 - second_decay) * gradient * gradient
    update = new_moment1 / first_fix / (jnp.sqrt(new_moment2 / second_fix) + epsilon)
    new_weight = (
        weight.astype(f32) * (1.0 - learning_rate * weight_decay) - learning_rate * update
    ).astype(bf16)
    return (new_weight, new_moment1, new_moment2)


def flip(value, axis, bit):
    return lax.ppermute(value, axis, [(i, i ^ bit) for i in range(lax.axis_size(axis))])


def to_partner(value):
    return flip(value, "dp", 1)


def to_chip(value):
    return flip(value, "tensor", 2)


def to_core(value):
    return flip(value, "tensor", 1)


def to_plane(value, bit):
    return flip(value, "dp", 2 * bit)


def stage(*values):
    return lax.optimization_barrier(values)


def relative(rows, x, c):
    block = rows.shape[0] // 4
    rows = rows.reshape(2, 2, block, rows.shape[1])
    rows = jnp.where(x == 1, rows[::-1], rows)
    rows = jnp.where(c == 1, rows[:, ::-1], rows)
    return rows.transpose(1, 0, 2, 3).reshape(4 * block, -1)


def absolute(rows, x, c):
    block = rows.shape[0] // 4
    rows = rows.reshape(2, 2, block, -1).transpose(1, 0, 2, 3)
    rows = jnp.where(c == 1, rows[:, ::-1], rows)
    rows = jnp.where(x == 1, rows[::-1], rows)
    return rows.reshape(4 * block, -1)


def params(mib):
    return pltpu.CompilerParams(vmem_limit_bytes=mib * 2**20)


def cost(flops, bytes_accessed):
    return pl.CostEstimate(flops=flops, bytes_accessed=bytes_accessed, transcendentals=0)


def gradient_kernel(scale, *refs):
    pieces, (saved0, saved1, out) = refs[:8], refs[8:]
    rows = saved0.shape[0]
    left = jnp.concatenate([ref[0] for ref in pieces], axis=1)
    total = jnp.dot(left[:, :rows], saved0[...], preferred_element_type=f32)
    total += jnp.dot(left[:, rows:], saved1[...], preferred_element_type=f32)
    out[...] = (total * scale).astype(bf16)


def gradient_part(pieces, saved0, saved1, index, scale):
    _, own, tok = pieces[0].shape
    rows, wide = saved0.shape
    steps = 2 if own % 32 == 0 else 1
    part = own // steps
    whole = pl.BlockSpec((rows, wide), lambda i: (0, 0))
    return pl.pallas_call(
        functools.partial(gradient_kernel, scale),
        grid=(steps,),
        in_specs=[pl.BlockSpec((1, part, tok), lambda i: (index, i, 0))] * 8 + [whole] * 2,
        out_specs=pl.BlockSpec((part, wide), lambda i: (i, 0)),
        out_shape=jax.ShapeDtypeStruct((own, wide), bf16),
        compiler_params=params(12),
        cost_estimate=cost(4 * own * rows * wide, 2 * own * (2 * rows + wide) + 4 * rows * wide),
        name="gradient_part",
    )(*pieces, saved0, saved1)


def attn_kernel(*refs):
    pieces, (weights, kept, sent, total) = refs[:8], refs[8:]
    step = pl.program_id(0)
    rows = kept.shape[0]
    left = jnp.concatenate([ref[0] for ref in pieces], axis=1)
    product = lax.dot_general(left, weights[0], (((0,), (0,)), ((), ())), preferred_element_type=f32)

    @pl.when(step == 0)
    def _():
        total[...] = product

    @pl.when(step > 0)
    def _():
        total[...] += product

    @pl.when(step == pl.num_programs(0) - 1)
    def _():
        kept[...] = total[:rows]
        sent[...] = total[rows:].astype(bf16)


def attn_part(pieces, weights):
    n, own, tok = pieces[0].shape
    wide = weights.shape[2]
    rows = 4 * tok
    whole = pl.BlockSpec((rows, wide), lambda i: (0, 0))
    return pl.pallas_call(
        attn_kernel,
        grid=(n,),
        in_specs=[pl.BlockSpec((1, own, tok), lambda i: (i, 0, 0))] * 8
        + [pl.BlockSpec((1, own, wide), lambda i: (i, 0, 0))],
        out_specs=[whole, whole],
        out_shape=[jax.ShapeDtypeStruct((rows, wide), f32), jax.ShapeDtypeStruct((rows, wide), bf16)],
        scratch_shapes=[pltpu.VMEM((2 * rows, wide), f32)],
        compiler_params=params(24),
        cost_estimate=cost(4 * n * own * rows * wide, 2 * n * own * (2 * rows + wide) + 6 * rows * wide),
        name="attn_part",
    )(*pieces, weights)


def outward_kernel(block, next0, next1, kept, sent):
    tok = kept.shape[3]
    for y, following in enumerate((next0, next1)):
        out = lax.dot_general(
            block[...], following[...], (((1,), (1,)), ((), ())), preferred_element_type=f32
        ).astype(bf16)
        for chip in range(2):
            kept[chip, y] = out[:, chip * tok : (chip + 1) * tok]
            sent[chip, y] = out[:, (2 + chip) * tok : (3 + chip) * tok]


def outward_part(block, next0, next1):
    own, wide = block.shape
    rows = next0.shape[0]
    shape = jax.ShapeDtypeStruct((2, 2, own, rows // 4), bf16)
    return pl.pallas_call(
        outward_kernel,
        out_shape=[shape, shape],
        compiler_params=params(12),
        cost_estimate=cost(4 * own * rows * wide, 2 * (own * wide + 2 * rows * wide + 2 * own * rows)),
        name="outward_part",
    )(block, next0, next1)


def add(a, b):
    return (a.astype(f32) + b.astype(f32)).astype(bf16)


def local(cotangent, attn_saved, attn_next, weight, moment1, moment2):
    dp, t = lax.axis_index("dp"), lax.axis_index("tensor")
    n = lax.axis_size("dp") // 2
    z, y, x, c = dp // 2, dp % 2, t // 2, t % 2
    own, wide = weight.shape
    tok = cotangent.shape[0]
    scale = 1.0 / math.sqrt(4 * tok * lax.axis_size("dp"))
    order = [n - 1] + [r for r in range(1, n - 1)] + [0]
    top = n // 2
    levels = [[r for r in range(n) if r.bit_count() == k] for k in range(n.bit_length())]

    weights = {0: weight}
    for r in reversed(levels[1]):
        weights[r] = to_plane(weight, r)

    blocks = cotangent.T.reshape(n, 2, own, tok)
    blocks = jnp.take(blocks, z ^ jnp.array(order), axis=0)
    mine = jnp.where(y == 0, blocks[:, 0], blocks[:, 1])
    other = jnp.where(y == 0, blocks[:, 1], blocks[:, 0])
    mine, other = stage(mine, other)
    partner = to_partner(other)
    mine_x = to_chip(mine)
    mine_c = to_core(mine)
    saved0 = relative(attn_saved, x, c)
    partner, mine_x, mine_c, saved0 = stage(partner, mine_x, mine_c, saved0)

    saved1 = to_partner(saved0)
    partner_x = to_chip(partner)
    partner_c = to_core(partner)
    came, saved1, partner_c, mine_x = stage([weights[r] for r in levels[1]], saved1, partner_c, mine_x)
    weights.update(zip(levels[1], came))
    mine_xc = to_core(mine_x)
    partner_x, mine_xc = stage(partner_x, mine_xc)
    for level in levels[2:]:
        for r in level:
            weights[r] = to_plane(weights[r & (r - 1)], r & -r)
    partner_xc = to_core(partner_x)
    pieces = [mine, mine_x, mine_c, mine_xc, partner, partner_x, partner_c, partner_xc]

    sums = {}
    for j, r in enumerate(order):
        sums[r] = gradient_part(pieces, saved0, saved1, j, scale)
    next0 = relative(attn_next, x, c)
    next1 = to_partner(next0)
    m = 1
    while m < top:
        sends = [r for r in sums if r & m and r != m]
        came = [to_plane(sums.pop(r), m) for r in sends]
        came, sums[m] = stage(came, sums[m])
        for r, value in zip(sends, came):
            sums[r ^ m] = add(sums[r ^ m], value)
        m *= 2
    ends = [1 << k for k in reversed(range(n.bit_length() - 1))]
    gathered, _ = stage([weights[r] for r in order], came)
    gathered = jnp.stack(gathered)
    came = [to_plane(sums[m], m) for m in ends]
    kept, sent = attn_part(pieces, gathered)
    came, next1, attn = stage(came, next1, [kept, sent])
    gradient = sums[0].astype(f32) + functools.reduce(jnp.add, [v.astype(f32) for v in came])
    new_weight, new_moment1, new_moment2 = adamw_step(gradient, weight, moment1, moment2)

    held, results = {0: new_weight}, {}
    for k, wave in enumerate(levels):
        later = levels[k + 1] if k + 1 < len(levels) else []
        for r in reversed(later):
            held[r] = to_plane(held[r & (r - 1)], r & -r)
        kept, came = {}, {}
        for r in wave:
            block, sent = outward_part(held[r], next0, next1)
            half = add(block, to_core(sent))
            kept[r], came[r] = half[0], to_chip(half[1])
        if later:
            blocks, kept = stage([held[r] for r in later], kept)
            if k == 0:
                attn = [attn[0], to_partner(attn[1])]
            blocks, came, results, attn = stage(blocks, came, results, attn)
            held.update(zip(later, blocks))
        for r in wave:
            total = add(kept[r], came[r])
            results[r] = (total[0], to_partner(total[1]))

    grad_attn = absolute((attn[0] + attn[1].astype(f32)).astype(bf16), x, c)
    mine = jnp.stack([results[r][0] for r in range(n)])
    other = jnp.stack([results[r][1] for r in range(n)])
    both = jnp.stack([jnp.where(y == 0, mine, other), jnp.where(y == 0, other, mine)], axis=1)
    next_out = jnp.take(both, z ^ jnp.arange(n), axis=0).reshape(2 * n * own, tok).T
    return (grad_attn, new_weight, new_moment1, new_moment2, next_out)


def solution(mesh):
    return jax.shard_map(
        local,
        mesh=mesh,
        in_specs=(
            P(("dp", "tensor"), None),
            P("dp", "tensor"),
            P("dp", "tensor"),
            P("dp", "tensor"),
            P("dp", "tensor"),
            P("dp", "tensor"),
        ),
        out_specs=(
            P("dp", "tensor"),
            P("dp", "tensor"),
            P("dp", "tensor"),
            P("dp", "tensor"),
            P(("dp", "tensor"), None),
        ),
        check_vma=False,
    )
```
